32 devices in a mesh: seq: 8 (over z, x), chan: 4 (over y, core).
Axes of the slice: x: 2, y: 2, z: 4, core: 2. Of those that a mesh axis runs over, the one named last changes fastest.
Arguments:
- signal: bfloat16 [2048, 1024], P('chan', 'seq'), may hold values from -6 to 6
- filters: float32 [2048, 1024], P('chan', 'seq'), may hold values from -1 to 1
- skip: float32 [2048], P('chan'), may hold values from 0.5 to 2
- weight: bfloat16 [2048, 8192], P(None, 'chan'), may hold values from -0.125 to 0.125
Outputs:
- mixed: bfloat16 [1024, 8192], P('seq', 'chan')
The draws below stay inside these ranges and needn't reach their ends.
All inputs are finite; a program needn't handle non-finite values.
Results may differ from the reference program's by a relative error of at most 0.0049.
Values may be sent and summed in bfloat16 or wider, within the bound.
A program may use at most 128 MiB of HBM per device.

```python
import math
import jax
import jax.numpy as jnp
from jax import lax

D = 8192
TOK_DEV = 128
CHANNELS = 2048
SEQ_LEN = 1024


def draw_filters(key, part):
    key_pick, key_rate, key_noise, key_floor = jax.random.split(jax.random.fold_in(key, 17), 4)
    steps_pos = jnp.arange(SEQ_LEN, dtype=jnp.float32)
    slow_share = 0.5
    is_slow = jax.random.uniform(key_pick, (CHANNELS, 1)) < slow_share
    level = jax.random.uniform(key_rate, (CHANNELS, 1))
    slow_rate = jnp.exp(jnp.log(0.2 / SEQ_LEN) + level * jnp.log(10.0))
    fast_rate = jnp.exp(jnp.log(1.0 / 40.0) + level * jnp.log(1.0 / 8.0))
    rate = jnp.where(is_slow, slow_rate, fast_rate)
    floor_level = 0.03 + 0.05 * jax.random.uniform(key_floor, (CHANNELS, 1))
    envelope = jnp.exp(-rate * steps_pos[None, :]) + floor_level
    scale_norm = jnp.sqrt(jnp.sum(envelope * envelope, axis=1, keepdims=True))
    noise = jnp.clip(jax.random.normal(key_noise, (CHANNELS, SEQ_LEN)), -4.0, 4.0)
    return (noise * envelope / scale_norm).astype(jnp.float32)


def steps_of(stream_key, extent, cuts, smallest, largest):
    factor_of, own = 1.0, jax.random.fold_in(stream_key, 6)
    for axis_at, shards_of in cuts:
        steps = jnp.exp(jax.random.uniform(jax.random.fold_in(own, axis_at), (shards_of,), jnp.float32, smallest / len(cuts), largest / len(cuts)))
        factor_of = factor_of * jnp.repeat(steps, extent[axis_at] // shards_of).reshape([-1 if axis == axis_at else 1 for axis in range(len(extent))])
    return factor_of


def scatter_about(rng, shape, deviation, reach, cuts=(), kind=jnp.bfloat16):
    gain = steps_of(rng, shape, cuts, -0.22, 0.18) if cuts else 1.0
    result = jax.random.normal(rng, shape, jnp.float32) * deviation * gain
    return jnp.minimum(jnp.maximum(result, -reach), reach).astype(kind)


def setup_inputs(seed: int = 0) -> dict:
    arg_keys = jax.random.split(jax.random.key(seed), 5)
    return {
        "signal": scatter_about(arg_keys[0], (CHANNELS, SEQ_LEN), 1.0, 6.0, ((0, 4), (1, 8))),
        "filters": draw_filters(jax.random.fold_in(arg_keys[4], 71), 0),
        "skip": jnp.clip(jnp.exp(math.log(2.0) - 1.3862944 * jax.random.uniform(arg_keys[2], (CHANNELS,), jnp.float32) ** steps_of(arg_keys[2], (CHANNELS,), ((0, 4),), -0.2, 0.2)), 0.5, 2.0),
        "weight": scatter_about(arg_keys[3], (CHANNELS, D), CHANNELS ** -0.5, 0.125, ((1, 4),)),
    }


def reference(signal, filters, skip, weight):
    length = signal.shape[1]
    padded_len = 2 * length
    source = signal.astype(jnp.float32)
    spec_signal = jnp.fft.rfft(source, n=padded_len, axis=1)
    spec_filter = jnp.fft.rfft(filters, n=padded_len, axis=1)
    conv = jnp.fft.irfft(spec_signal * spec_filter, n=padded_len, axis=1)[:, :length]
    conv = conv + skip[:, None] * source
    filtered = conv.astype(jnp.bfloat16)
    token_rows = filtered.T.reshape(length // TOK_DEV, TOK_DEV, filtered.shape[0])

    def project(piece_rows):
        return jnp.dot(piece_rows, weight, preferred_element_type=jnp.float32).astype(jnp.bfloat16)

    blocks = lax.map(project, token_rows)
    return blocks.reshape(length, weight.shape[1])
```

```python
import functools

import jax
import jax.numpy as jnp
from jax import lax
from jax.experimental import pallas as pl
from jax.experimental.pallas import tpu as pltpu
from jax.sharding import PartitionSpec as P

MESH = pl.DeviceIdType.MESH
VMEM = pl.BlockSpec(memory_space=pltpu.VMEM)
LIMIT = 48 * 1024 * 1024


def greet(peers):
    barrier = pltpu.get_barrier_semaphore()
    for peer in peers:
        pl.semaphore_signal(barrier, inc=1, device_id=peer, device_id_type=MESH)
    pl.semaphore_wait(barrier, len(peers))


def scatter_kernel(groups, signal_ref, filter_ref, out_ref, cast, send_sem, recv_sem):
    me = lax.axis_index("seq")
    own = signal_ref.shape[0] // groups
    peers = [lax.rem(me + k, groups) for k in range(1, groups)]
    greet([{"seq": peer} for peer in peers])
    copies = []

    def send(which, source):
        for k, peer in enumerate(peers):
            copy = pltpu.make_async_remote_copy(
                src_ref=source.at[pl.ds(peer * own, own)],
                dst_ref=out_ref.at[k + 1, which],
                send_sem=send_sem.at[which, k],
                recv_sem=recv_sem.at[which, k],
                device_id={"seq": peer},
                device_id_type=MESH,
            )
            copy.start()
            copies.append(copy)

    send(0, signal_ref)
    cast[...] = filter_ref[...].astype(cast.dtype)
    send(1, cast)
    out_ref[0, 0] = signal_ref[pl.ds(me * own, own), :]
    out_ref[0, 1] = cast[pl.ds(me * own, own), :]
    for copy in copies:
        copy.wait()


def conv_kernel(groups, skip_ref, blocks_ref, out_ref, taps, source, result):
    me = lax.axis_index("seq")
    own, tokens = blocks_ref.shape[2:]
    for k in range(groups):
        place = lax.rem(me - k + groups, groups)
        source[:, place, :] = blocks_ref[k, 0].astype(jnp.float32)
        taps[:, place, :] = blocks_ref[k, 1].astype(jnp.float32)
    row = lax.broadcasted_iota(jnp.int32, (tokens, tokens), 0)
    lane = lax.broadcasted_iota(jnp.int32, (tokens, tokens), 1)
    at_or_after = lane >= row
    token_block = lax.broadcasted_iota(jnp.int32, (groups, tokens), 0)

    def toeplitz(channel):
        rows = taps[channel]
        parts = []
        before = jnp.zeros((tokens, tokens), jnp.float32)
        for d in range(groups):
            turned = pltpu.roll(
                jnp.broadcast_to(rows[d : d + 1, :], (tokens, tokens)),
                0,
                1,
                stride=1,
                stride_axis=0,
            )
            parts.append(jnp.where(at_or_after, turned, before).astype(jnp.bfloat16))
            before = turned
        return jnp.concatenate(parts, axis=0)

    def shifted(values):
        parts = [values]
        for d in range(1, groups):
            moved = pltpu.roll(values, d, 0)
            parts.append(jnp.where(token_block >= d, moved, 0.0))
        return jnp.concatenate(parts, axis=1)

    def pair(step, carry):
        first = 2 * step
        second = first + 1
        one, two = source[first], source[second]
        left = jnp.concatenate([shifted(one), shifted(two)], axis=0).astype(jnp.bfloat16)
        right = jnp.concatenate([toeplitz(first), toeplitz(second)], axis=1)
        both = jnp.dot(left, right, preferred_element_type=jnp.float32)
        result[first] = both[:groups, :tokens] + skip_ref[me * own + first] * one
        result[second] = both[groups:, tokens:] + skip_ref[me * own + second] * two
        return carry

    lax.fori_loop(0, own // 2, pair, 0)
    for k in range(groups):
        out_ref[k] = result[:, k, :].astype(out_ref.dtype)


def project_kernel(
    groups, lanes, values_ref, weight_ref, out_ref, gathered, held, left,
    seq_send, seq_recv, chan_send, chan_recv, pass_send, pass_recv, weight_sem,
):
    me = lax.axis_index("seq")
    lane = lax.axis_index("chan")
    own, tokens = values_ref.shape[1:]
    sibling = lane + 1 - 2 * lax.rem(lane, 2)
    others = [lax.rem(lane + 2 * j, lanes) for j in range(1, lanes // 2)]
    partners = [lax.rem(me + k, groups) for k in range(1, groups)]
    load = pltpu.make_async_copy(weight_ref, held, weight_sem)
    load.start()
    greet(
        [{"seq": peer} for peer in partners]
        + [{"chan": other} for other in others]
        + [{"chan": sibling}]
    )
    sent = []

    def push(source, target, send_sem, recv_sem, device):
        copy = pltpu.make_async_remote_copy(
            src_ref=source,
            dst_ref=target,
            send_sem=send_sem,
            recv_sem=recv_sem,
            device_id=device,
            device_id_type=MESH,
        )
        copy.start()
        sent.append(copy)
        return copy

    slot = lambda which, at: gathered.at[which, at]
    arrivals = []
    for k, peer in enumerate(partners):
        arrivals.append(
            push(values_ref.at[peer], slot(lane, me), seq_send.at[k], seq_recv.at[k], {"seq": peer})
        )
    gathered[lane, me] = values_ref[me]
    crossing = []
    inside = []
    for k in range(groups):
        at = lax.rem(me - k + groups, groups)
        if k:
            arrivals[k - 1].wait_recv()
        for j, other in enumerate(others):
            crossing.append((j, at, k, push(
                slot(lane, at), slot(lane, at), chan_send.at[j, k], chan_recv.at[j, k],
                {"chan": other})))
        inside.append(push(
            slot(lane, at), slot(lane, at), pass_send.at[0, k], pass_recv.at[0, k],
            {"chan": sibling}))
    for j, at, k, copy in crossing:
        copy.wait_recv()
        origin = lax.rem(lane - 2 * (j + 1) + lanes, lanes)
        inside.append(push(
            slot(origin, at), slot(origin, at), pass_send.at[j + 1, k], pass_recv.at[j + 1, k],
            {"chan": sibling}))
    for copy in inside:
        copy.wait_recv()
    for copy in sent:
        copy.wait_send()
    depth = lanes * groups * own
    left[...] = gathered[...].reshape(depth, tokens).T
    load.wait()
    wide = 512 if out_ref.shape[1] % 512 == 0 else out_ref.shape[1]

    def tile(step, carry):
        columns = pl.ds(pl.multiple_of(step * wide, wide), wide)
        out_ref[:, columns] = jnp.dot(
            left[...], held[:, columns], preferred_element_type=jnp.float32
        ).astype(out_ref.dtype)
        return carry

    lax.fori_loop(0, out_ref.shape[1] // wide, tile, 0)


def per_device(signal, filters, skip, weight):
    groups = lax.axis_size("seq")
    lanes = lax.axis_size("chan")
    channels, tokens = signal.shape
    own = channels // groups
    half = jnp.bfloat16
    dma = pltpu.SemaphoreType.DMA
    blocks = pl.pallas_call(
        functools.partial(scatter_kernel, groups),
        out_shape=jax.ShapeDtypeStruct((groups, 2, own, tokens), half),
        in_specs=[VMEM, VMEM],
        out_specs=VMEM,
        scratch_shapes=[
            pltpu.VMEM((channels, tokens), half),
            dma((2, groups - 1)),
            dma((2, groups - 1)),
        ],
        compiler_params=pltpu.CompilerParams(
            collective_id=0, has_side_effects=True, vmem_limit_bytes=LIMIT
        ),
    )(signal, filters)
    values = pl.pallas_call(
        functools.partial(conv_kernel, groups),
        out_shape=jax.ShapeDtypeStruct((groups, own, tokens), half),
        in_specs=[pl.BlockSpec(memory_space=pltpu.SMEM), VMEM],
        out_specs=VMEM,
        scratch_shapes=[pltpu.VMEM((own, groups, tokens), jnp.float32)] * 3,
        compiler_params=pltpu.CompilerParams(vmem_limit_bytes=LIMIT),
    )(skip, blocks)
    return pl.pallas_call(
        functools.partial(project_kernel, groups, lanes),
        out_shape=jax.ShapeDtypeStruct((tokens, weight.shape[1]), half),
        in_specs=[VMEM, pl.BlockSpec(memory_space=pl.ANY)],
        out_specs=VMEM,
        scratch_shapes=[
            pltpu.VMEM((lanes, groups, own, tokens), half),
            pltpu.VMEM(weight.shape, half),
            pltpu.VMEM((tokens, weight.shape[0]), half),
            dma((groups - 1,)),
            dma((groups - 1,)),
            dma((max(lanes // 2 - 1, 1), groups)),
            dma((max(lanes // 2 - 1, 1), groups)),
            dma((lanes // 2, groups)),
            dma((lanes // 2, groups)),
            dma,
        ],
        compiler_params=pltpu.CompilerParams(
            collective_id=1, has_side_effects=True, vmem_limit_bytes=LIMIT
        ),
    )(values, weight)


def solution(mesh):
    in_specs = (P("chan", "seq"), P("chan", "seq"), P("chan"), P(None, "chan"))
    out_specs = P("seq", "chan")
    return jax.shard_map(
        per_device, mesh=mesh, in_specs=in_specs, out_specs=out_specs, check_vma=False
    )
```

```python
import functools

import jax
import jax.numpy as jnp
from jax import lax
from jax.experimental import pallas as pl
from jax.experimental.pallas import tpu as pltpu
from jax.sharding import PartitionSpec as P

MESH = pl.DeviceIdType.MESH
VMEM = pl.BlockSpec(memory_space=pltpu.VMEM)
PARTS = 2
LIMIT = 64 * 1024 * 1024


def greet(peers):
    barrier = pltpu.get_barrier_semaphore()
    for peer in peers:
        pl.semaphore_signal(barrier, inc=1, device_id=peer, device_id_type=MESH)
    pl.semaphore_wait(barrier, len(peers))


class Toeplitz:
    def __init__(self, groups, tokens):
        self.groups, self.tokens = groups, tokens
        row = lax.broadcasted_iota(jnp.int32, (16, tokens), 0)
        lane = lax.broadcasted_iota(jnp.int32, (16, tokens), 1)
        self.at_or_after = lane >= row
        self.lane = lax.broadcasted_iota(jnp.int16, (16, tokens), 1)
        self.block = lax.broadcasted_iota(jnp.int32, (groups, tokens), 0)

    def matrix(self, rows):
        tokens = self.tokens
        parts = []
        before = jnp.zeros((16, tokens), jnp.float32)
        base_before = jnp.zeros((16, tokens), jnp.bfloat16)
        for d in range(self.groups):
            turned = pltpu.roll(
                jnp.broadcast_to(rows[d : d + 1, :], (16, tokens)), 0, 1, stride=1, stride_axis=0
            )
            base = jnp.where(self.at_or_after, turned, before).astype(jnp.bfloat16)
            parts.append(base)
            for start in range(16, tokens, 16):
                window = jnp.where(self.lane < tokens - start, base, base_before)
                parts.append(pltpu.roll(window, start, 1))
            before, base_before = turned, base
        return jnp.concatenate(parts, axis=0)

    def shifted(self, values):
        parts = [values]
        for d in range(1, self.groups):
            parts.append(jnp.where(self.block >= d, pltpu.roll(values, d, 0), 0.0))
        return jnp.concatenate(parts, axis=1)


def layer_kernel(
    groups, lanes, parts, signal_ref, filter_ref, skip_ref, weight_ref, out_ref,
    raw, cast, gains, recv, source, taps, result, values, gathered, held, left, total,
    load_sem, split_send, split_recv, seq_send, seq_recv,
    chan_send, chan_recv, pass_send, pass_recv,
):
    me = lax.axis_index("seq")
    lane = lax.axis_index("chan")
    tokens = signal_ref.shape[1]
    own = signal_ref.shape[0] // groups
    part = own // parts
    sibling = lane + 1 - 2 * lax.rem(lane, 2)
    others = [lax.rem(lane + 2 * j, lanes) for j in range(1, lanes // 2)]
    partners = [lax.rem(me + k, groups) for k in range(1, groups)]

    filter_load = pltpu.make_async_copy(filter_ref, raw, load_sem.at[0])
    skip_load = pltpu.make_async_copy(skip_ref, gains, load_sem.at[1])
    weight_load = pltpu.make_async_copy(weight_ref, held, load_sem.at[2])
    own_loads = [
        pltpu.make_async_copy(
            signal_ref.at[pl.ds(me * own + h * part, part)], recv.at[h, 0, 0], load_sem.at[3 + h]
        )
        for h in range(parts)
    ]
    filter_load.start()
    for load in own_loads:
        load.start()
    skip_load.start()
    greet(
        [{"seq": peer} for peer in partners]
        + [{"chan": other} for other in others]
        + [{"chan": sibling}]
    )
    sent = []

    def push(origin, target, send_sem, recv_sem, device):
        copy = pltpu.make_async_remote_copy(
            src_ref=origin,
            dst_ref=target,
            send_sem=send_sem,
            recv_sem=recv_sem,
            device_id=device,
            device_id_type=MESH,
        )
        copy.start()
        sent.append(copy)
        return copy

    def split(h, which, origin):
        return [
            push(
                origin.at[pl.ds(peer * own + h * part, part)],
                recv.at[h, k + 1, which],
                split_send.at[h, which, k],
                split_recv.at[h, which, k],
                {"seq": peer},
            )
            for k, peer in enumerate(partners)
        ]

    tools = Toeplitz(groups, tokens)

    def unpack(h):
        for k in range(groups):
            place = lax.rem(me - k + groups, groups)
            source[:, place, :] = recv[h, k, 0].astype(jnp.float32)
            taps[:, place, :] = recv[h, k, 1].astype(jnp.float32)

    def convolve(h, begin, end):
        def pair(step, carry):
            first = 2 * step
            second = first + 1
            one, two = source[first], source[second]
            rows = jnp.concatenate([tools.shifted(one), tools.shifted(two)], axis=0)
            columns = jnp.concatenate(
                [tools.matrix(taps[first]), tools.matrix(taps[second])], axis=1
            )
            both = jnp.dot(
                rows.astype(jnp.bfloat16), columns, preferred_element_type=jnp.float32
            )
            base = me * own + h * part
            result[first] = both[:groups, :tokens] + gains[base + first] * one
            result[second] = both[groups:, tokens:] + gains[base + second] * two
            return carry

        lax.fori_loop(begin, end, pair, 0)

    def pack(h):
        for k in range(groups):
            values[h, k] = result[:, k, :].astype(values.dtype)

    def slot(h, which, at):
        return gathered.at[h, which, at]

    def send_values(h):
        copies = [
            push(
                values.at[h, peer], slot(h, lane, me), seq_send.at[h, k], seq_recv.at[h, k],
                {"seq": peer},
            )
            for k, peer in enumerate(partners)
        ]
        gathered[h, lane, me] = values[h, me]
        return copies

    def spread(h, arrivals):
        crossing, inside = [], []
        for k in range(groups):
            at = lax.rem(me - k + groups, groups)
            if k:
                arrivals[k - 1].wait_recv()
            for j, other in enumerate(others):
                crossing.append((j, k, push(
                    slot(h, lane, at), slot(h, lane, at),
                    chan_send.at[h, j, k], chan_recv.at[h, j, k], {"chan": other},
                )))
            inside.append(push(
                slot(h, lane, at), slot(h, lane, at),
                pass_send.at[h, 0, k], pass_recv.at[h, 0, k], {"chan": sibling},
            ))
        return crossing, inside

    def hand_over(h, crossing, inside):
        for j, k, copy in crossing:
            copy.wait_recv()
            at = lax.rem(me - k + groups, groups)
            origin = lax.rem(lane - 2 * (j + 1) + lanes, lanes)
            inside.append(push(
                slot(h, origin, at), slot(h, origin, at),
                pass_send.at[h, j + 1, k], pass_recv.at[h, j + 1, k], {"chan": sibling},
            ))

    wide = 512 if out_ref.shape[1] % 512 == 0 else out_ref.shape[1]
    tiles = out_ref.shape[1] // wide
    depth = lanes * groups * part

    def settle(h, inside):
        for copy in inside:
            copy.wait_recv()
        left[...] = gathered[h].reshape(depth, tokens).T

    def project(h, begin, end):
        def tile(step, carry):
            columns = pl.ds(pl.multiple_of(step * wide, wide), wide)
            block = held[:, h * part : (h + 1) * part, columns].reshape(depth, wide)
            amount = jnp.dot(left[...], block, preferred_element_type=jnp.float32)
            if h:
                amount = amount + total[:, columns]
            if h == parts - 1:
                out_ref[:, columns] = amount.astype(out_ref.dtype)
            else:
                total[:, columns] = amount
            return carry

        lax.fori_loop(begin, end, tile, 0)

    incoming = [split(0, 0, signal_ref)]
    filter_load.wait()
    cast[...] = raw[...].astype(cast.dtype)
    incoming.append(split(0, 1, cast))
    for h in range(parts):
        recv[h, 0, 1] = cast[pl.ds(me * own + h * part, part), :]
    skip_load.wait()
    weight_load.start()
    pairs = part // 2
    arrivals = crossing = inside = None
    for h in range(parts):
        own_loads[h].wait()
        for copies in incoming:
            for copy in copies:
                copy.wait_recv()
        if h + 1 < parts:
            incoming = [split(h + 1, 0, signal_ref), split(h + 1, 1, cast)]
        unpack(h)
        if h:
            convolve(h, 0, pairs // 2)
            crossing, inside = spread(h - 1, arrivals)
            convolve(h, pairs // 2, pairs)
            hand_over(h - 1, crossing, inside)
        else:
            convolve(h, 0, pairs)
        pack(h)
        arrivals = send_values(h)
        if h == 1:
            weight_load.wait()
        if h:
            settle(h - 1, inside)
            project(h - 1, 0, tiles // 2)
    last = parts - 1
    crossing, inside = spread(last, arrivals)
    if last:
        project(last - 1, tiles // 2, tiles)
    else:
        weight_load.wait()
    hand_over(last, crossing, inside)
    settle(last, inside)
    project(last, 0, tiles)
    for copy in sent:
        copy.wait_send()


def per_device(signal, filters, skip, weight):
    groups = lax.axis_size("seq")
    lanes = lax.axis_size("chan")
    channels, tokens = signal.shape
    features = weight.shape[1]
    own = channels // groups
    parts = PARTS if own % (16 * PARTS) == 0 else 1
    part = own // parts
    across = max(lanes // 2 - 1, 1)
    half, full = jnp.bfloat16, jnp.float32
    dma = pltpu.SemaphoreType.DMA
    whole = pl.BlockSpec(memory_space=pltpu.HBM)
    return pl.pallas_call(
        functools.partial(layer_kernel, groups, lanes, parts),
        out_shape=jax.ShapeDtypeStruct((tokens, features), half),
        in_specs=[whole] * 4,
        out_specs=VMEM,
        scratch_shapes=[
            pltpu.VMEM((channels, tokens), full),
            pltpu.VMEM((channels, tokens), half),
            pltpu.SMEM((channels,), full),
            pltpu.VMEM((parts, groups, 2, part, tokens), half),
            pltpu.VMEM((part, groups, tokens), full),
            pltpu.VMEM((part, groups, tokens), full),
            pltpu.VMEM((part, groups, tokens), full),
            pltpu.VMEM((parts, groups, part, tokens), half),
            pltpu.VMEM((parts, lanes, groups, part, tokens), half),
            pltpu.VMEM((lanes * groups, own, features), half),
            pltpu.VMEM((tokens, lanes * groups * part), half),
            pltpu.VMEM((tokens, features), full),
            dma((3 + parts,)),
            dma((parts, 2, groups - 1)),
            dma((parts, 2, groups - 1)),
            dma((parts, groups - 1)),
            dma((parts, groups - 1)),
            dma((parts, across, groups)),
            dma((parts, across, groups)),
            dma((parts, lanes // 2, groups)),
            dma((parts, lanes // 2, groups)),
        ],
        compiler_params=pltpu.CompilerParams(
            collective_id=0, has_side_effects=True, vmem_limit_bytes=LIMIT
        ),
    )(signal, filters, skip, weight.reshape(lanes * groups, own, features))


def solution(mesh):
    in_specs = (P("chan", "seq"), P("chan", "seq"), P("chan"), P(None, "chan"))
    out_specs = P("seq", "chan")
    return jax.shard_map(
        per_device, mesh=mesh, in_specs=in_specs, out_specs=out_specs, check_vma=False
    )
```

```python
import functools

import jax
import jax.numpy as jnp
from jax import lax
from jax.experimental import pallas as pl
from jax.experimental.pallas import tpu as pltpu
from jax.sharding import PartitionSpec as P

MESH = pl.DeviceIdType.MESH
VMEM = pl.BlockSpec(memory_space=pltpu.VMEM)
PARTS = 2
SHARE = 4
LIMIT = 64 * 1024 * 1024


def greet(peers):
    barrier = pltpu.get_barrier_semaphore()
    for peer in peers:
        pl.semaphore_signal(barrier, inc=1, device_id=peer, device_id_type=MESH)
    pl.semaphore_wait(barrier, len(peers))


class Toeplitz:
    def __init__(self, groups, tokens, width):
        self.groups, self.tokens = groups, tokens
        self.width, self.count = width, tokens // width
        row = lax.broadcasted_iota(jnp.int32, (width, tokens), 0)
        lane = lax.broadcasted_iota(jnp.int32, (width, tokens), 1)
        self.inside = lax.rem(lane, width) < width - row
        self.lane = lax.broadcasted_iota(jnp.int32, (groups, tokens), 1)
        self.piece = self.lane // width
        self.row = lax.broadcasted_iota(jnp.int32, (groups, tokens), 0)

    def turn(self, value, pieces):
        pieces = pieces % self.count
        return pltpu.roll(value, pieces * self.width, 1) if pieces else value

    def gather(self, pick):
        value = pick(0)
        for p in range(1, self.count):
            value = jnp.where(self.piece == p, pick(p), value)
        return value

    def down(self, value):
        return jnp.where(self.row >= 1, pltpu.roll(value, 1, 0), 0.0)

    def matrix(self, taps):
        count, width, tokens = self.count, self.width, self.tokens
        here = [
            self.gather(lambda g, e=e: self.turn(taps[g], g - e)) for e in range(count)
        ]
        following = [self.turn(value, -1) for value in here]
        before = [self.down(following[-1])] + following[:-1]
        parts = []
        for d in range(self.groups):
            for e in reversed(range(count)):
                near = jnp.broadcast_to(here[e][d : d + 1, :], (width, tokens))
                far = jnp.broadcast_to(before[e][d : d + 1, :], (width, tokens))
                tile = pltpu.roll(
                    jnp.where(self.inside, near, far), 0, 1, stride=1, stride_axis=0
                )
                parts.append(tile.astype(jnp.bfloat16))
        return jnp.concatenate(parts, axis=0)

    def windows(self, value):
        previous = self.down(value)
        views = []
        for b in range(self.count):
            back = self.count - 1 - b
            kept = jnp.where(self.piece < self.count - back, value, previous)
            views.append(self.turn(kept, back))
        return views


def layer_kernel(
    groups, lanes, parts, signal_ref, filter_ref, skip_ref, weight_ref, out_ref,
    raw, cast, gains, recv, source, taps, result, padded, values, gathered, held, left, total,
    load_sem, split_send, split_recv, seq_send, seq_recv,
    chan_send, chan_recv, pass_send, pass_recv,
):
    me = lax.axis_index("seq")
    lane = lax.axis_index("chan")
    tokens = signal_ref.shape[1]
    own = signal_ref.shape[0] // groups
    part = own // parts
    sibling = lane + 1 - 2 * lax.rem(lane, 2)
    others = [lax.rem(lane + 2 * j, lanes) for j in range(1, lanes // 2)]
    partners = [lax.rem(me + k, groups) for k in range(1, groups)]

    filter_load = pltpu.make_async_copy(filter_ref, raw, load_sem.at[0])
    skip_load = pltpu.make_async_copy(skip_ref, gains, load_sem.at[1])
    weight_load = pltpu.make_async_copy(weight_ref, held, load_sem.at[2])
    own_loads = [
        pltpu.make_async_copy(
            signal_ref.at[pl.ds(me * own + h * part, part)], recv.at[h, 0, 0], load_sem.at[3 + h]
        )
        for h in range(parts)
    ]
    filter_load.start()
    for load in own_loads:
        load.start()
    skip_load.start()
    greet(
        [{"seq": peer} for peer in partners]
        + [{"chan": other} for other in others]
        + [{"chan": sibling}]
    )
    sent = []

    def push(origin, target, send_sem, recv_sem, device):
        copy = pltpu.make_async_remote_copy(
            src_ref=origin,
            dst_ref=target,
            send_sem=send_sem,
            recv_sem=recv_sem,
            device_id=device,
            device_id_type=MESH,
        )
        copy.start()
        sent.append(copy)
        return copy

    def split(h, which, origin):
        return [
            push(
                origin.at[pl.ds(peer * own + h * part, part)],
                recv.at[h, k + 1, which],
                split_send.at[h, which, k],
                split_recv.at[h, which, k],
                {"seq": peer},
            )
            for k, peer in enumerate(partners)
        ]

    tools = Toeplitz(groups, tokens, tokens // SHARE)

    def unpack(h):
        for k in range(groups):
            place = lax.rem(me - k + groups, groups)
            rows = pl.ds(pl.multiple_of(place * part, part), part)
            source[rows, :] = recv[h, k, 0].astype(jnp.float32)
            taps[rows, :] = recv[h, k, 1].astype(jnp.float32)

    def convolve(h, begin, end):
        def several(step, carry):
            first = step * SHARE
            picks = [pl.ds(first + g, groups, stride=part) for g in range(SHARE)]
            inputs = [source[pick, :] for pick in picks]
            for g in range(SHARE):
                for b, view in enumerate(tools.windows(inputs[g])):
                    padded[g * SHARE + b, groups:, :] = view
            rows = jnp.concatenate(
                [
                    padded[:, groups - d : 2 * groups - d, :]
                    .reshape(SHARE * SHARE * groups, tokens)
                    .astype(jnp.bfloat16)
                    for d in range(groups)
                ],
                axis=1,
            )
            columns = tools.matrix([taps[pick, :] for pick in picks])
            both = jnp.dot(rows, columns, preferred_element_type=jnp.float32)
            both = both.reshape(SHARE, SHARE, groups, tokens)
            base = me * own + h * part + first
            for g, pick in enumerate(picks):
                joined = tools.gather(lambda b, g=g: tools.turn(both[g, b], b - g))
                result[pick, :] = joined + gains[base + g] * inputs[g]
            return carry

        lax.fori_loop(begin, end, several, 0)

    def pack(h):
        for k in range(groups):
            values[h, k] = result[k * part : (k + 1) * part, :].astype(values.dtype)

    def slot(h, which, at):
        return gathered.at[h, which, at]

    def send_values(h):
        copies = [
            push(
                values.at[h, peer], slot(h, lane, me), seq_send.at[h, k], seq_recv.at[h, k],
                {"seq": peer},
            )
            for k, peer in enumerate(partners)
        ]
        gathered[h, lane, me] = values[h, me]
        return copies

    def spread(h, arrivals):
        crossing, inside = [], []
        for k in range(groups):
            at = lax.rem(me - k + groups, groups)
            if k:
                arrivals[k - 1].wait_recv()
            for j, other in enumerate(others):
                crossing.append((j, k, push(
                    slot(h, lane, at), slot(h, lane, at),
                    chan_send.at[h, j, k], chan_recv.at[h, j, k], {"chan": other},
                )))
            inside.append(push(
                slot(h, lane, at), slot(h, lane, at),
                pass_send.at[h, 0, k], pass_recv.at[h, 0, k], {"chan": sibling},
            ))
        return crossing, inside

    def hand_over(h, crossing, inside):
        for j, k, copy in crossing:
            copy.wait_recv()
            at = lax.rem(me - k + groups, groups)
            origin = lax.rem(lane - 2 * (j + 1) + lanes, lanes)
            inside.append(push(
                slot(h, origin, at), slot(h, origin, at),
                pass_send.at[h, j + 1, k], pass_recv.at[h, j + 1, k], {"chan": sibling},
            ))

    wide = 512 if out_ref.shape[1] % 512 == 0 else out_ref.shape[1]
    tiles = out_ref.shape[1] // wide
    depth = lanes * groups * part

    def settle(h, inside):
        for copy in inside:
            copy.wait_recv()
        left[...] = gathered[h].reshape(depth, tokens).T

    def project(h, begin, end):
        def tile(step, carry):
            columns = pl.ds(pl.multiple_of(step * wide, wide), wide)
            block = held[:, h * part : (h + 1) * part, columns].reshape(depth, wide)
            amount = jnp.dot(left[...], block, preferred_element_type=jnp.float32)
            if h:
                amount = amount + total[:, columns]
            if h == parts - 1:
                out_ref[:, columns] = amount.astype(out_ref.dtype)
            else:
                total[:, columns] = amount
            return carry

        lax.fori_loop(begin, end, tile, 0)

    incoming = [split(0, 0, signal_ref)]
    filter_load.wait()
    cast[...] = raw[...].astype(cast.dtype)
    incoming.append(split(0, 1, cast))
    for h in range(parts):
        recv[h, 0, 1] = cast[pl.ds(me * own + h * part, part), :]
    skip_load.wait()
    padded[:, :groups, :] = jnp.zeros((SHARE * SHARE, groups, tokens), jnp.float32)
    weight_load.start()
    turns = part // SHARE
    arrivals = crossing = inside = None
    for h in range(parts):
        own_loads[h].wait()
        for copies in incoming:
            for copy in copies:
                copy.wait_recv()
        if h + 1 < parts:
            incoming = [split(h + 1, 0, signal_ref), split(h + 1, 1, cast)]
        unpack(h)
        if h:
            convolve(h, 0, turns // 2)
            crossing, inside = spread(h - 1, arrivals)
            convolve(h, turns // 2, turns)
            hand_over(h - 1, crossing, inside)
        else:
            convolve(h, 0, turns)
        pack(h)
        arrivals = send_values(h)
        if h == 1:
            weight_load.wait()
        if h:
            settle(h - 1, inside)
            project(h - 1, 0, tiles // 2)
    last = parts - 1
    crossing, inside = spread(last, arrivals)
    if last:
        project(last - 1, tiles // 2, tiles)
    else:
        weight_load.wait()
    hand_over(last, crossing, inside)
    settle(last, inside)
    project(last, 0, tiles)
    for copy in sent:
        copy.wait_send()


def per_device(signal, filters, skip, weight):
    groups = lax.axis_size("seq")
    lanes = lax.axis_size("chan")
    channels, tokens = signal.shape
    features = weight.shape[1]
    own = channels // groups
    parts = PARTS if own % (16 * PARTS) == 0 else 1
    part = own // parts
    across = max(lanes // 2 - 1, 1)
    half, full = jnp.bfloat16, jnp.float32
    dma = pltpu.SemaphoreType.DMA
    whole = pl.BlockSpec(memory_space=pltpu.HBM)
    return pl.pallas_call(
        functools.partial(layer_kernel, groups, lanes, parts),
        out_shape=jax.ShapeDtypeStruct((tokens, features), half),
        in_specs=[whole] * 4,
        out_specs=VMEM,
        scratch_shapes=[
            pltpu.VMEM((channels, tokens), full),
            pltpu.VMEM((channels, tokens), half),
            pltpu.SMEM((channels,), full),
            pltpu.VMEM((parts, groups, 2, part, tokens), half),
            pltpu.VMEM((groups * part, tokens), full),
            pltpu.VMEM((groups * part, tokens), full),
            pltpu.VMEM((groups * part, tokens), full),
            pltpu.VMEM((SHARE * SHARE, 2 * groups, tokens), full),
            pltpu.VMEM((parts, groups, part, tokens), half),
            pltpu.VMEM((parts, lanes, groups, part, tokens), half),
            pltpu.VMEM((lanes * groups, own, features), half),
            pltpu.VMEM((tokens, lanes * groups * part), half),
            pltpu.VMEM((tokens, features), full),
            dma((3 + parts,)),
            dma((parts, 2, groups - 1)),
            dma((parts, 2, groups - 1)),
            dma((parts, groups - 1)),
            dma((parts, groups - 1)),
            dma((parts, across, groups)),
            dma((parts, across, groups)),
            dma((parts, lanes // 2, groups)),
            dma((parts, lanes // 2, groups)),
        ],
        compiler_params=pltpu.CompilerParams(
            collective_id=0, has_side_effects=True, vmem_limit_bytes=LIMIT
        ),
    )(signal, filters, skip, weight.reshape(lanes * groups, own, features))


def solution(mesh):
    in_specs = (P("chan", "seq"), P("chan", "seq"), P("chan"), P(None, "chan"))
    out_specs = P("seq", "chan")
    return jax.shard_map(
        per_device, mesh=mesh, in_specs=in_specs, out_specs=out_specs, check_vma=False
    )
```

```python
import functools

import jax
import jax.numpy as jnp
from jax import lax
from jax.experimental import pallas as pl
from jax.experimental.pallas import tpu as pltpu
from jax.sharding import PartitionSpec as P

MESH = pl.DeviceIdType.MESH
VMEM = pl.BlockSpec(memory_space=pltpu.VMEM)
PARTS = 2
SHARE = 4
ROOMS = 2
LIMIT = 64 * 1024 * 1024


def greet(peers):
    barrier = pltpu.get_barrier_semaphore()
    for peer in peers:
        pl.semaphore_signal(barrier, inc=1, device_id=peer, device_id_type=MESH)
    pl.semaphore_wait(barrier, len(peers))


class Toeplitz:
    def __init__(self, groups, tokens, width):
        self.groups, self.tokens = groups, tokens
        self.width, self.count = width, tokens // width
        row = lax.broadcasted_iota(jnp.int32, (width, tokens), 0)
        lane = lax.broadcasted_iota(jnp.int32, (width, tokens), 1)
        self.inside = lax.rem(lane, width) < width - row
        self.lane = lax.broadcasted_iota(jnp.int32, (groups, tokens), 1)
        self.piece = self.lane // width
        self.row = lax.broadcasted_iota(jnp.int32, (groups, tokens), 0)

    def turn(self, value, pieces):
        pieces = pieces % self.count
        return pltpu.roll(value, pieces * self.width, 1) if pieces else value

    def gather(self, pick):
        value = pick(0)
        for p in range(1, self.count):
            value = jnp.where(self.piece == p, pick(p), value)
        return value

    def down(self, value):
        return jnp.where(self.row >= 1, pltpu.roll(value, 1, 0), 0.0)

    def matrix(self, taps):
        count, width, tokens = self.count, self.width, self.tokens
        here = [
            self.gather(lambda g, e=e: self.turn(taps[g], g - e)) for e in range(count)
        ]
        following = [self.turn(value, -1) for value in here]
        before = [self.down(following[-1])] + following[:-1]
        parts = []
        for d in range(self.groups):
            for e in reversed(range(count)):
                near = jnp.broadcast_to(here[e][d : d + 1, :], (width, tokens))
                far = jnp.broadcast_to(before[e][d : d + 1, :], (width, tokens))
                tile = pltpu.roll(
                    jnp.where(self.inside, near, far), 0, 1, stride=1, stride_axis=0
                )
                parts.append(tile.astype(jnp.bfloat16))
        return jnp.concatenate(parts, axis=0)

    def windows(self, value):
        previous = self.down(value)
        views = []
        for b in range(self.count):
            back = self.count - 1 - b
            kept = jnp.where(self.piece < self.count - back, value, previous)
            views.append(self.turn(kept, back))
        return views


def layer_kernel(
    groups, lanes, parts, signal_ref, filter_ref, skip_ref, weight_ref, out_ref,
    raw, stage, gains, recv, source, taps, result, padded, values, gathered, held, left, total,
    load_sem, split_send, split_recv, seq_send, seq_recv,
    chan_send, chan_recv, pass_send, pass_recv,
):
    me = lax.axis_index("seq")
    lane = lax.axis_index("chan")
    part, tokens = signal_ref.shape[2:]
    own = parts * part
    sibling = lane + 1 - 2 * lax.rem(lane, 2)
    others = [lax.rem(lane + 2 * j, lanes) for j in range(1, lanes // 2)]
    partners = [lax.rem(me + k, groups) for k in range(1, groups)]

    filter_load = pltpu.make_async_copy(filter_ref, raw, load_sem.at[0])
    skip_load = pltpu.make_async_copy(skip_ref, gains, load_sem.at[1])
    weight_load = pltpu.make_async_copy(weight_ref, held, load_sem.at[2])
    signal_loads = [
        pltpu.make_async_copy(signal_ref.at[:, h], stage.at[h, :, 0], load_sem.at[3 + h])
        for h in range(parts)
    ]
    filter_load.start()
    for load in signal_loads:
        load.start()
    skip_load.start()
    greet(
        [{"seq": peer} for peer in partners]
        + [{"chan": other} for other in others]
        + [{"chan": sibling}]
    )
    sent = []

    def push(origin, target, send_sem, recv_sem, device):
        copy = pltpu.make_async_remote_copy(
            src_ref=origin,
            dst_ref=target,
            send_sem=send_sem,
            recv_sem=recv_sem,
            device_id=device,
            device_id_type=MESH,
        )
        copy.start()
        sent.append(copy)
        return copy

    def split(h):
        return [
            push(
                stage.at[h, peer], recv.at[h, k + 1], split_send.at[h, k], split_recv.at[h, k],
                {"seq": peer},
            )
            for k, peer in enumerate(partners)
        ]

    tools = Toeplitz(groups, tokens, tokens // SHARE)

    def unpack(h):
        for k in range(groups):
            place = lax.rem(me - k + groups, groups)
            rows = pl.ds(pl.multiple_of(place * part, part), part)
            source[rows, :] = recv[h, k, 0].astype(jnp.float32)
            taps[rows, :] = recv[h, k, 1].astype(jnp.float32)

    def convolve(h, begin, end):
        def several(first, room):
            picks = [pl.ds(first + g, groups, stride=part) for g in range(SHARE)]
            inputs = [source[pick, :] for pick in picks]
            for g in range(SHARE):
                for b, view in enumerate(tools.windows(inputs[g])):
                    padded[room, g * SHARE + b, groups:, :] = view
            rows = jnp.concatenate(
                [
                    padded[room, :, groups - d : 2 * groups - d, :]
                    .reshape(SHARE * SHARE * groups, tokens)
                    .astype(jnp.bfloat16)
                    for d in range(groups)
                ],
                axis=1,
            )
            columns = tools.matrix([taps[pick, :] for pick in picks])
            both = jnp.dot(rows, columns, preferred_element_type=jnp.float32)
            both = both.reshape(SHARE, SHARE, groups, tokens)
            base = me * own + h * part + first
            return [
                (pick, tools.gather(lambda b, g=g: tools.turn(both[g, b], b - g))
                 + gains[base + g] * inputs[g])
                for g, pick in enumerate(picks)
            ]

        def turn(step, carry):
            done = []
            for room in range(ROOMS):
                done += several((step * ROOMS + room) * SHARE, room)
            for pick, value in done:
                result[pick, :] = value
            return carry

        lax.fori_loop(begin, end, turn, 0)

    def pack(h):
        for k in range(groups):
            values[h, k] = result[k * part : (k + 1) * part, :].astype(values.dtype)

    def slot(h, which, at):
        return gathered.at[h, which, at]

    def send_values(h):
        copies = [
            push(
                values.at[h, peer], slot(h, lane, me), seq_send.at[h, k], seq_recv.at[h, k],
                {"seq": peer},
            )
            for k, peer in enumerate(partners)
        ]
        gathered[h, lane, me] = values[h, me]
        return copies

    def hand(h, which, send_sem, recv_sem, device):
        row = gathered.at[h, which]
        return push(row, row, send_sem, recv_sem, device)

    def spread(h, arrivals):
        for copy in arrivals:
            copy.wait_recv()
        crossing = [
            hand(h, lane, chan_send.at[h, j], chan_recv.at[h, j], {"chan": other})
            for j, other in enumerate(others)
        ]
        inside = [hand(h, lane, pass_send.at[h, 0], pass_recv.at[h, 0], {"chan": sibling})]
        return crossing, inside

    def hand_over(h, crossing, inside):
        for j, copy in enumerate(crossing):
            copy.wait_recv()
            origin = lax.rem(lane - 2 * (j + 1) + lanes, lanes)
            inside.append(hand(
                h, origin, pass_send.at[h, j + 1], pass_recv.at[h, j + 1], {"chan": sibling}
            ))

    wide = 512 if out_ref.shape[1] % 512 == 0 else out_ref.shape[1]
    tiles = out_ref.shape[1] // wide
    depth = lanes * groups * part

    def settle(h, inside):
        for copy in inside:
            copy.wait_recv()
        left[...] = gathered[h].reshape(depth, tokens).T

    def project(h, begin, end):
        def tile(step, carry):
            columns = pl.ds(pl.multiple_of(step * wide, wide), wide)
            block = held[:, h * part : (h + 1) * part, columns].reshape(depth, wide)
            amount = jnp.dot(left[...], block, preferred_element_type=jnp.float32)
            if h:
                amount = amount + total[:, columns]
            if h == parts - 1:
                out_ref[:, columns] = amount.astype(out_ref.dtype)
            else:
                total[:, columns] = amount
            return carry

        lax.fori_loop(begin, end, tile, 0)

    filter_load.wait()
    stage[:, :, 1] = jnp.swapaxes(raw[...].astype(stage.dtype), 0, 1)
    signal_loads[0].wait()
    incoming = split(0)
    skip_load.wait()
    padded[:, :, :groups, :] = jnp.zeros((ROOMS, SHARE * SHARE, groups, tokens), jnp.float32)
    weight_load.start()
    turns = part // (SHARE * ROOMS)
    arrivals = crossing = inside = None
    for h in range(parts):
        recv[h, 0] = stage[h, me]
        for copy in incoming:
            copy.wait_recv()
        if h + 1 < parts:
            signal_loads[h + 1].wait()
            incoming = split(h + 1)
        unpack(h)
        if h:
            convolve(h, 0, turns // 2)
            crossing, inside = spread(h - 1, arrivals)
            convolve(h, turns // 2, turns)
            hand_over(h - 1, crossing, inside)
        else:
            convolve(h, 0, turns)
        pack(h)
        arrivals = send_values(h)
        if h == 1:
            weight_load.wait()
        if h:
            settle(h - 1, inside)
            project(h - 1, 0, tiles // 2)
    last = parts - 1
    crossing, inside = spread(last, arrivals)
    if last:
        project(last - 1, tiles // 2, tiles)
    else:
        weight_load.wait()
    hand_over(last, crossing, inside)
    settle(last, inside)
    project(last, 0, tiles)
    for copy in sent:
        copy.wait_send()


def per_device(signal, filters, skip, weight):
    groups = lax.axis_size("seq")
    lanes = lax.axis_size("chan")
    channels, tokens = signal.shape
    features = weight.shape[1]
    own = channels // groups
    parts = PARTS if own % (16 * PARTS) == 0 else 1
    part = own // parts
    across = max(lanes // 2 - 1, 1)
    half, full = jnp.bfloat16, jnp.float32
    dma = pltpu.SemaphoreType.DMA
    whole = pl.BlockSpec(memory_space=pltpu.HBM)
    return pl.pallas_call(
        functools.partial(layer_kernel, groups, lanes, parts),
        out_shape=jax.ShapeDtypeStruct((tokens, features), half),
        in_specs=[whole] * 4,
        out_specs=VMEM,
        scratch_shapes=[
            pltpu.VMEM((groups, parts, part, tokens), full),
            pltpu.VMEM((parts, groups, 2, part, tokens), half),
            pltpu.SMEM((channels,), full),
            pltpu.VMEM((parts, groups, 2, part, tokens), half),
            pltpu.VMEM((groups * part, tokens), full),
            pltpu.VMEM((groups * part, tokens), full),
            pltpu.VMEM((groups * part, tokens), full),
            pltpu.VMEM((ROOMS, SHARE * SHARE, 2 * groups, tokens), full),
            pltpu.VMEM((parts, groups, part, tokens), half),
            pltpu.VMEM((parts, lanes, groups, part, tokens), half),
            pltpu.VMEM((lanes * groups, own, features), half),
            pltpu.VMEM((tokens, lanes * groups * part), half),
            pltpu.VMEM((tokens, features), full),
            dma((3 + parts,)),
            dma((parts, groups - 1)),
            dma((parts, groups - 1)),
            dma((parts, groups - 1)),
            dma((parts, groups - 1)),
            dma((parts, across)),
            dma((parts, across)),
            dma((parts, lanes // 2)),
            dma((parts, lanes // 2)),
        ],
        compiler_params=pltpu.CompilerParams(
            collective_id=0, has_side_effects=True, vmem_limit_bytes=LIMIT
        ),
    )(
        signal.reshape(groups, parts, part, tokens),
        filters.reshape(groups, parts, part, tokens),
        skip,
        weight.reshape(lanes * groups, own, features),
    )


def solution(mesh):
    in_specs = (P("chan", "seq"), P("chan", "seq"), P("chan"), P(None, "chan"))
    out_specs = P("seq", "chan")
    return jax.shard_map(
        per_device, mesh=mesh, in_specs=in_specs, out_specs=out_specs, check_vma=False
    )
```

```python
import functools

import jax
import jax.numpy as jnp
from jax import lax
from jax.experimental import pallas as pl
from jax.experimental.pallas import tpu as pltpu
from jax.sharding import PartitionSpec as P

MESH = pl.DeviceIdType.MESH
VMEM = pl.BlockSpec(memory_space=pltpu.VMEM)
PARTS = 4
SHARE = 4
ROOMS = 2
LIMIT = 64 * 1024 * 1024


def greet(peers):
    barrier = pltpu.get_barrier_semaphore()
    for peer in peers:
        pl.semaphore_signal(barrier, inc=1, device_id=peer, device_id_type=MESH)
    pl.semaphore_wait(barrier, len(peers))


class Toeplitz:
    def __init__(self, groups, tokens, width):
        self.groups, self.tokens = groups, tokens
        self.width, self.count = width, tokens // width
        row = lax.broadcasted_iota(jnp.int32, (width, tokens), 0)
        lane = lax.broadcasted_iota(jnp.int32, (width, tokens), 1)
        self.inside = lax.rem(lane, width) < width - row
        self.lane = lax.broadcasted_iota(jnp.int32, (groups, tokens), 1)
        self.piece = self.lane // width
        self.row = lax.broadcasted_iota(jnp.int32, (groups, tokens), 0)

    def turn(self, value, pieces):
        pieces = pieces % self.count
        return pltpu.roll(value, pieces * self.width, 1) if pieces else value

    def gather(self, pick):
        value = pick(0)
        for p in range(1, self.count):
            value = jnp.where(self.piece == p, pick(p), value)
        return value

    def down(self, value):
        return jnp.where(self.row >= 1, pltpu.roll(value, 1, 0), 0.0)

    def matrix(self, taps):
        count, width, tokens = self.count, self.width, self.tokens
        here = [
            self.gather(lambda g, e=e: self.turn(taps[g], g - e)) for e in range(count)
        ]
        following = [self.turn(value, -1) for value in here]
        before = [self.down(following[-1])] + following[:-1]
        parts = []
        for d in range(self.groups):
            for e in reversed(range(count)):
                near = jnp.broadcast_to(here[e][d : d + 1, :], (width, tokens))
                far = jnp.broadcast_to(before[e][d : d + 1, :], (width, tokens))
                tile = pltpu.roll(
                    jnp.where(self.inside, near, far), 0, 1, stride=1, stride_axis=0
                )
                parts.append(tile.astype(jnp.bfloat16))
        return jnp.concatenate(parts, axis=0)

    def windows(self, value):
        previous = self.down(value)
        views = []
        for b in range(self.count):
            back = self.count - 1 - b
            kept = jnp.where(self.piece < self.count - back, value, previous)
            views.append(self.turn(kept, back))
        return views


def layer_kernel(
    groups, lanes, parts, signal_ref, filter_ref, skip_ref, weight_ref, out_ref,
    raw, stage, gains, recv, source, taps, result, padded, values, gathered, held, left, total,
    load_sem, split_send, split_recv, seq_send, seq_recv,
    chan_send, chan_recv,
):
    me = lax.axis_index("seq")
    lane = lax.axis_index("chan")
    part, tokens = signal_ref.shape[2:]
    own = parts * part
    others = [lax.rem(lane + j, lanes) for j in range(1, lanes)]
    partners = [lax.rem(me + k, groups) for k in range(1, groups)]

    filter_load = pltpu.make_async_copy(filter_ref, raw, load_sem.at[0])
    skip_load = pltpu.make_async_copy(skip_ref, gains, load_sem.at[1])
    weight_load = pltpu.make_async_copy(weight_ref, held, load_sem.at[2])
    signal_loads = [
        pltpu.make_async_copy(signal_ref.at[:, h], stage.at[h, :, 0], load_sem.at[3 + h])
        for h in range(parts)
    ]
    filter_load.start()
    for load in signal_loads:
        load.start()
    skip_load.start()
    greet(
        [{"seq": peer} for peer in partners]
        + [{"chan": other} for other in others]
    )
    sent = []

    def push(origin, target, send_sem, recv_sem, device):
        copy = pltpu.make_async_remote_copy(
            src_ref=origin,
            dst_ref=target,
            send_sem=send_sem,
            recv_sem=recv_sem,
            device_id=device,
            device_id_type=MESH,
        )
        copy.start()
        sent.append(copy)
        return copy

    def split(h):
        return [
            push(
                stage.at[h, peer], recv.at[h, k + 1], split_send.at[h, k], split_recv.at[h, k],
                {"seq": peer},
            )
            for k, peer in enumerate(partners)
        ]

    tools = Toeplitz(groups, tokens, tokens // SHARE)

    def unpack(h):
        for k in range(groups):
            place = lax.rem(me - k + groups, groups)
            rows = pl.ds(pl.multiple_of(place * part, part), part)
            source[rows, :] = recv[h, k, 0].astype(jnp.float32)
            taps[rows, :] = recv[h, k, 1].astype(jnp.float32)

    def convolve(h, begin, end):
        def several(first, room):
            picks = [pl.ds(first + g, groups, stride=part) for g in range(SHARE)]
            inputs = [source[pick, :] for pick in picks]
            for g in range(SHARE):
                for b, view in enumerate(tools.windows(inputs[g])):
                    padded[room, g * SHARE + b, groups:, :] = view
            rows = jnp.concatenate(
                [
                    padded[room, :, groups - d : 2 * groups - d, :]
                    .reshape(SHARE * SHARE * groups, tokens)
                    .astype(jnp.bfloat16)
                    for d in range(groups)
                ],
                axis=1,
            )
            columns = tools.matrix([taps[pick, :] for pick in picks])
            both = jnp.dot(rows, columns, preferred_element_type=jnp.float32)
            both = both.reshape(SHARE, SHARE, groups, tokens)
            base = me * own + h * part + first
            return [
                (pick, tools.gather(lambda b, g=g: tools.turn(both[g, b], b - g))
                 + gains[base + g] * inputs[g])
                for g, pick in enumerate(picks)
            ]

        def turn(step, carry):
            done = []
            for room in range(ROOMS):
                done += several((step * ROOMS + room) * SHARE, room)
            for pick, value in done:
                result[pick, :] = value
            return carry

        lax.fori_loop(begin, end, turn, 0)

    def pack(h):
        for k in range(groups):
            values[h, k] = result[k * part : (k + 1) * part, :].astype(values.dtype)

    def slot(h, which, at):
        return gathered.at[h, which, at]

    def send_values(h):
        copies = [
            push(
                values.at[h, peer], slot(h, lane, me), seq_send.at[h, k], seq_recv.at[h, k],
                {"seq": peer},
            )
            for k, peer in enumerate(partners)
        ]
        gathered[h, lane, me] = values[h, me]
        return copies

    def hand(h, which, send_sem, recv_sem, device):
        row = gathered.at[h, which]
        return push(row, row, send_sem, recv_sem, device)

    def spread(h, arrivals):
        for copy in arrivals:
            copy.wait_recv()
        row = gathered.at[h, lane]
        return [
            push(row, row, chan_send.at[h, j], chan_recv.at[h, j], {"chan": other})
            for j, other in enumerate(others)
        ]

    wide = 512 if out_ref.shape[1] % 512 == 0 else out_ref.shape[1]
    tiles = out_ref.shape[1] // wide
    depth = lanes * groups * part

    def settle(h, inside):
        for copy in inside:
            copy.wait_recv()
        left[...] = gathered[h].reshape(depth, tokens).T

    def project(h, begin, end):
        def tile(step, carry):
            columns = pl.ds(pl.multiple_of(step * wide, wide), wide)
            block = held[:, h * part : (h + 1) * part, columns].reshape(depth, wide)
            amount = jnp.dot(left[...], block, preferred_element_type=jnp.float32)
            if h:
                amount = amount + total[:, columns]
            if h == parts - 1:
                out_ref[:, columns] = amount.astype(out_ref.dtype)
            else:
                total[:, columns] = amount
            return carry

        lax.fori_loop(begin, end, tile, 0)

    filter_load.wait()
    stage[:, :, 1] = jnp.swapaxes(raw[...].astype(stage.dtype), 0, 1)
    signal_loads[0].wait()
    incoming = [split(0)]
    skip_load.wait()
    padded[:, :, :groups, :] = jnp.zeros((ROOMS, SHARE * SHARE, groups, tokens), jnp.float32)
    if parts > 1:
        signal_loads[1].wait()
        incoming.append(split(1))
    weight_load.start()
    turns = part // (SHARE * ROOMS)
    arrivals, inside = [], []
    for h in range(parts):
        recv[h, 0] = stage[h, me]
        for copy in incoming[h]:
            copy.wait_recv()
        if h + 2 < parts:
            signal_loads[h + 2].wait()
            incoming.append(split(h + 2))
        unpack(h)
        convolve(h, 0, turns)
        pack(h)
        arrivals.append(send_values(h))
        if h == 1:
            weight_load.wait()
        if h >= 1:
            inside.append(spread(h - 1, arrivals[h - 1]))
        if h >= 2 and h < parts - 1:
            settle(h - 2, inside[h - 2])
            project(h - 2, 0, tiles)
    last = parts - 1
    if last == 0:
        weight_load.wait()
    if last >= 2:
        settle(last - 2, inside[last - 2])
        project(last - 2, 0, tiles)
    inside.append(spread(last, arrivals[last]))
    if last >= 1:
        settle(last - 1, inside[last - 1])
        project(last - 1, 0, tiles)
    settle(last, inside[last])
    project(last, 0, tiles)
    for copy in sent:
        copy.wait_send()


def per_device(signal, filters, skip, weight):
    groups = lax.axis_size("seq")
    lanes = lax.axis_size("chan")
    channels, tokens = signal.shape
    features = weight.shape[1]
    own = channels // groups
    parts = PARTS if own % (16 * PARTS) == 0 else 1
    part = own // parts
    half, full = jnp.bfloat16, jnp.float32
    dma = pltpu.SemaphoreType.DMA
    whole = pl.BlockSpec(memory_space=pltpu.HBM)
    sums = pl.pallas_call(
        functools.partial(layer_kernel, groups, lanes, parts),
        out_shape=jax.ShapeDtypeStruct((tokens, features), full),
        in_specs=[whole] * 4,
        out_specs=VMEM,
        scratch_shapes=[
            pltpu.VMEM((groups, parts, part, tokens), full),
            pltpu.VMEM((parts, groups, 2, part, tokens), half),
            pltpu.SMEM((channels,), full),
            pltpu.VMEM((parts, groups, 2, part, tokens), half),
            pltpu.VMEM((groups * part, tokens), full),
            pltpu.VMEM((groups * part, tokens), full),
            pltpu.VMEM((groups * part, tokens), full),
            pltpu.VMEM((ROOMS, SHARE * SHARE, 2 * groups, tokens), full),
            pltpu.VMEM((parts, groups, part, tokens), half),
            pltpu.VMEM((parts, lanes, groups, part, tokens), half),
            pltpu.VMEM((lanes * groups, own, features), half),
            pltpu.VMEM((tokens, lanes * groups * part), half),
            pltpu.VMEM((tokens, features), full),
            dma((3 + parts,)),
            dma((parts, groups - 1)),
            dma((parts, groups - 1)),
            dma((parts, groups - 1)),
            dma((parts, groups - 1)),
            dma((parts, lanes - 1)),
            dma((parts, lanes - 1)),
        ],
        compiler_params=pltpu.CompilerParams(
            collective_id=0, has_side_effects=True, vmem_limit_bytes=LIMIT
        ),
    )(
        signal.reshape(groups, parts, part, tokens),
        filters.reshape(groups, parts, part, tokens),
        skip,
        weight.reshape(lanes * groups, own, features),
    )
    return sums.astype(half)


def solution(mesh):
    in_specs = (P("chan", "seq"), P("chan", "seq"), P("chan"), P(None, "chan"))
    out_specs = P("seq", "chan")
    return jax.shard_map(
        per_device, mesh=mesh, in_specs=in_specs, out_specs=out_specs, check_vma=False
    )
```

```python
import functools

import jax
import jax.numpy as jnp
from jax import lax
from jax.experimental import pallas as pl
from jax.experimental.pallas import tpu as pltpu
from jax.sharding import PartitionSpec as P

MESH = pl.DeviceIdType.MESH
VMEM = pl.BlockSpec(memory_space=pltpu.VMEM)
PARTS = 4
SHARE = 4
ROOMS = 2
LIMIT = 64 * 1024 * 1024


def greet(peers):
    barrier = pltpu.get_barrier_semaphore()
    for peer in peers:
        pl.semaphore_signal(barrier, inc=1, device_id=peer, device_id_type=MESH)
    pl.semaphore_wait(barrier, len(peers))


class Toeplitz:
    def __init__(self, groups, tokens, width):
        self.groups, self.tokens = groups, tokens
        self.width, self.count = width, tokens // width
        self.lane = lax.broadcasted_iota(jnp.int32, (groups, tokens), 1)
        self.piece = self.lane // width
        self.inside = lax.rem(self.lane, width)
        self.row = lax.broadcasted_iota(jnp.int32, (groups, tokens), 0)

    def turn(self, value, pieces):
        pieces = pieces % self.count
        return pltpu.roll(value, pieces * self.width, 1) if pieces else value

    def gather(self, pick):
        value = pick(0)
        for p in range(1, self.count):
            value = jnp.where(self.piece == p, pick(p), value)
        return value

    def down(self, value):
        return jnp.where(self.row >= 1, pltpu.roll(value, 1, 0), 0.0)

    def matrix(self, taps, held):
        count, width, groups = self.count, self.width, self.groups
        here = [
            self.gather(lambda g, e=e: self.turn(taps[g], g - e)) for e in range(count)
        ]
        following = [self.turn(value, -1) for value in here]
        before = [self.down(following[-1])] + following[:-1]
        for e in range(count):
            for m in range(width):
                tile = here[e]
                if m:
                    tile = pltpu.roll(jnp.where(self.inside < width - m, tile, before[e]), m, 1)
                at = ((count - 1 - e) * width + m) * groups
                held[at : at + groups, :] = tile
        return jnp.concatenate(
            [
                held[pl.ds(d, count * width, stride=groups), :].astype(jnp.bfloat16)
                for d in range(groups)
            ],
            axis=0,
        )

    def windows(self, value):
        previous = self.down(value)
        views = []
        for b in range(self.count):
            back = self.count - 1 - b
            kept = jnp.where(self.piece < self.count - back, value, previous)
            views.append(self.turn(kept, back))
        return views


def layer_kernel(
    groups, lanes, parts, signal_ref, filter_ref, skip_ref, weight_ref, out_ref,
    raw, stage, gains, recv, source, taps, result, padded, tiles_held, values, gathered, held, left, total,
    load_sem, split_send, split_recv, seq_send, seq_recv,
    chan_send, chan_recv,
):
    me = lax.axis_index("seq")
    lane = lax.axis_index("chan")
    part, tokens = signal_ref.shape[2:]
    own = parts * part
    others = [lax.rem(lane + j, lanes) for j in range(1, lanes)]
    partners = [lax.rem(me + k, groups) for k in range(1, groups)]

    filter_load = pltpu.make_async_copy(filter_ref, raw, load_sem.at[0])
    skip_load = pltpu.make_async_copy(skip_ref, gains, load_sem.at[1])
    weight_load = pltpu.make_async_copy(weight_ref, held, load_sem.at[2])
    signal_loads = [
        pltpu.make_async_copy(signal_ref.at[:, h], stage.at[h, :, 0], load_sem.at[3 + h])
        for h in range(parts)
    ]
    filter_load.start()
    for load in signal_loads:
        load.start()
    skip_load.start()
    greet(
        [{"seq": peer} for peer in partners]
        + [{"chan": other} for other in others]
    )
    sent = []

    def push(origin, target, send_sem, recv_sem, device):
        copy = pltpu.make_async_remote_copy(
            src_ref=origin,
            dst_ref=target,
            send_sem=send_sem,
            recv_sem=recv_sem,
            device_id=device,
            device_id_type=MESH,
        )
        copy.start()
        sent.append(copy)
        return copy

    def split(h):
        return [
            push(
                stage.at[h, peer], recv.at[h, k + 1], split_send.at[h, k], split_recv.at[h, k],
                {"seq": peer},
            )
            for k, peer in enumerate(partners)
        ]

    tools = Toeplitz(groups, tokens, tokens // SHARE)

    def unpack(h):
        for k in range(groups):
            place = lax.rem(me - k + groups, groups)
            rows = pl.ds(pl.multiple_of(place * part, part), part)
            source[rows, :] = recv[h, k, 0].astype(jnp.float32)
            taps[rows, :] = recv[h, k, 1].astype(jnp.float32)

    def convolve(h, begin, end):
        def picks_of(first):
            return [pl.ds(first + g, groups, stride=part) for g in range(SHARE)]

        def rows_of(inputs, room):
            for g in range(SHARE):
                for b, view in enumerate(tools.windows(inputs[g])):
                    padded[room, g * SHARE + b, groups:, :] = view
            return jnp.concatenate(
                [
                    padded[room, :, groups - d : 2 * groups - d, :]
                    .reshape(SHARE * SHARE * groups, tokens)
                    .astype(jnp.bfloat16)
                    for d in range(groups)
                ],
                axis=1,
            )

        def turn(step, carry):
            firsts = [(step * ROOMS + room) * SHARE for room in range(ROOMS)]
            picks = [picks_of(first) for first in firsts]
            inputs = [[source[pick, :] for pick in several] for several in picks]
            rows = jnp.concatenate(
                [rows_of(inputs[room], room) for room in range(ROOMS)], axis=0
            )
            columns = jnp.concatenate(
                [
                    tools.matrix([taps[pick, :] for pick in picks[room]], tiles_held.at[room])
                    for room in range(ROOMS)
                ],
                axis=1,
            )
            product = jnp.dot(rows, columns, preferred_element_type=jnp.float32)
            height = SHARE * SHARE * groups
            for room in range(ROOMS):
                both = product[
                    room * height : (room + 1) * height, room * tokens : (room + 1) * tokens
                ].reshape(SHARE, SHARE, groups, tokens)
                base = me * own + h * part + firsts[room]
                for g, pick in enumerate(picks[room]):
                    joined = tools.gather(lambda b, g=g: tools.turn(both[g, b], b - g))
                    result[pick, :] = joined + gains[base + g] * inputs[room][g]
            return carry

        lax.fori_loop(begin, end, turn, 0)

    def pack(h):
        for k in range(groups):
            values[h, k] = result[k * part : (k + 1) * part, :].astype(values.dtype)

    def slot(h, which, at):
        return gathered.at[h, which, at]

    def send_values(h):
        copies = [
            push(
                values.at[h, peer], slot(h, lane, me), seq_send.at[h, k], seq_recv.at[h, k],
                {"seq": peer},
            )
            for k, peer in enumerate(partners)
        ]
        gathered[h, lane, me] = values[h, me]
        return copies

    def hand(h, which, send_sem, recv_sem, device):
        row = gathered.at[h, which]
        return push(row, row, send_sem, recv_sem, device)

    def spread(h, arrivals):
        for copy in arrivals:
            copy.wait_recv()
        row = gathered.at[h, lane]
        return [
            push(row, row, chan_send.at[h, j], chan_recv.at[h, j], {"chan": other})
            for j, other in enumerate(others)
        ]

    wide = 512 if out_ref.shape[1] % 512 == 0 else out_ref.shape[1]
    tiles = out_ref.shape[1] // wide
    depth = lanes * groups * part

    def settle(h, inside):
        for copy in inside:
            copy.wait_recv()
        left[...] = gathered[h].reshape(depth, tokens).T

    def project(h, begin, end):
        def tile(step, carry):
            columns = pl.ds(pl.multiple_of(step * wide, wide), wide)
            block = held[:, h * part : (h + 1) * part, columns].reshape(depth, wide)
            amount = jnp.dot(left[...], block, preferred_element_type=jnp.float32)
            if h:
                amount = amount + total[:, columns]
            if h == parts - 1:
                out_ref[:, columns] = amount.astype(out_ref.dtype)
            else:
                total[:, columns] = amount
            return carry

        lax.fori_loop(begin, end, tile, 0)

    filter_load.wait()
    stage[:, :, 1] = jnp.swapaxes(raw[...].astype(stage.dtype), 0, 1)
    signal_loads[0].wait()
    incoming = [split(0)]
    skip_load.wait()
    padded[:, :, :groups, :] = jnp.zeros((ROOMS, SHARE * SHARE, groups, tokens), jnp.float32)
    if parts > 1:
        signal_loads[1].wait()
        incoming.append(split(1))
    weight_load.start()
    turns = part // (SHARE * ROOMS)
    arrivals, inside = [], []
    for h in range(parts):
        recv[h, 0] = stage[h, me]
        for copy in incoming[h]:
            copy.wait_recv()
        if h + 2 < parts:
            signal_loads[h + 2].wait()
            incoming.append(split(h + 2))
        unpack(h)
        convolve(h, 0, turns)
        pack(h)
        arrivals.append(send_values(h))
        if h == 1:
            weight_load.wait()
        if h >= 1:
            inside.append(spread(h - 1, arrivals[h - 1]))
        if h >= 2 and h < parts - 1:
            settle(h - 2, inside[h - 2])
            project(h - 2, 0, tiles)
    last = parts - 1
    if last == 0:
        weight_load.wait()
    if last >= 2:
        settle(last - 2, inside[last - 2])
        project(last - 2, 0, tiles)
    inside.append(spread(last, arrivals[last]))
    if last >= 1:
        settle(last - 1, inside[last - 1])
        project(last - 1, 0, tiles)
    settle(last, inside[last])
    project(last, 0, tiles)
    for copy in sent:
        copy.wait_send()


def per_device(signal, filters, skip, weight):
    groups = lax.axis_size("seq")
    lanes = lax.axis_size("chan")
    channels, tokens = signal.shape
    features = weight.shape[1]
    own = channels // groups
    parts = PARTS if own % (16 * PARTS) == 0 else 1
    part = own // parts
    half, full = jnp.bfloat16, jnp.float32
    dma = pltpu.SemaphoreType.DMA
    whole = pl.BlockSpec(memory_space=pltpu.HBM)
    return pl.pallas_call(
        functools.partial(layer_kernel, groups, lanes, parts),
        out_shape=jax.ShapeDtypeStruct((tokens, features), half),
        in_specs=[whole] * 4,
        out_specs=VMEM,
        scratch_shapes=[
            pltpu.VMEM((groups, parts, part, tokens), full),
            pltpu.VMEM((parts, groups, 2, part, tokens), half),
            pltpu.SMEM((channels,), full),
            pltpu.VMEM((parts, groups, 2, part, tokens), half),
            pltpu.VMEM((groups * part, tokens), full),
            pltpu.VMEM((groups * part, tokens), full),
            pltpu.VMEM((groups * part, tokens), full),
            pltpu.VMEM((ROOMS, SHARE * SHARE, 2 * groups, tokens), full),
            pltpu.VMEM((ROOMS, groups * tokens, tokens), full),
            pltpu.VMEM((parts, groups, part, tokens), half),
            pltpu.VMEM((parts, lanes, groups, part, tokens), half),
            pltpu.VMEM((lanes * groups, own, features), half),
            pltpu.VMEM((tokens, lanes * groups * part), half),
            pltpu.VMEM((tokens, features), full),
            dma((3 + parts,)),
            dma((parts, groups - 1)),
            dma((parts, groups - 1)),
            dma((parts, groups - 1)),
            dma((parts, groups - 1)),
            dma((parts, lanes - 1)),
            dma((parts, lanes - 1)),
        ],
        compiler_params=pltpu.CompilerParams(
            collective_id=0, has_side_effects=True, vmem_limit_bytes=LIMIT
        ),
    )(
        signal.reshape(groups, parts, part, tokens),
        filters.reshape(groups, parts, part, tokens),
        skip,
        weight.reshape(lanes * groups, own, features),
    )


def solution(mesh):
    in_specs = (P("chan", "seq"), P("chan", "seq"), P("chan"), P(None, "chan"))
    out_specs = P("seq", "chan")
    return jax.shard_map(
        per_device, mesh=mesh, in_specs=in_specs, out_specs=out_specs, check_vma=False
    )
```

```python
import functools

import jax
import jax.numpy as jnp
from jax import lax
from jax.experimental import pallas as pl
from jax.experimental.pallas import tpu as pltpu
from jax.sharding import PartitionSpec as P

MESH = pl.DeviceIdType.MESH
VMEM = pl.BlockSpec(memory_space=pltpu.VMEM)
PARTS = 4
SHARE = 4
ROOMS = 2
LIMIT = 64 * 1024 * 1024


def greet(peers):
    barrier = pltpu.get_barrier_semaphore()
    for peer in peers:
        pl.semaphore_signal(barrier, inc=1, device_id=peer, device_id_type=MESH)
    pl.semaphore_wait(barrier, len(peers))


class Toeplitz:
    def __init__(self, groups, tokens, width):
        self.groups, self.tokens = groups, tokens
        self.width, self.count = width, tokens // width
        row = lax.broadcasted_iota(jnp.int32, (width, tokens), 0)
        lane = lax.broadcasted_iota(jnp.int32, (width, tokens), 1)
        self.inside = lax.rem(lane, width) < width - row
        self.lane = lax.broadcasted_iota(jnp.int32, (groups, tokens), 1)
        self.piece = self.lane // width
        self.row = lax.broadcasted_iota(jnp.int32, (groups, tokens), 0)

    def turn(self, value, pieces):
        pieces = pieces % self.count
        return pltpu.roll(value, pieces * self.width, 1) if pieces else value

    def gather(self, pick):
        value = pick(0)
        for p in range(1, self.count):
            value = jnp.where(self.piece == p, pick(p), value)
        return value

    def down(self, value):
        return jnp.where(self.row >= 1, pltpu.roll(value, 1, 0), 0.0)

    def matrix(self, taps):
        count, width, tokens = self.count, self.width, self.tokens
        here = [
            self.gather(lambda g, e=e: self.turn(taps[g], g - e)) for e in range(count)
        ]
        following = [self.turn(value, -1) for value in here]
        before = [self.down(following[-1])] + following[:-1]
        parts = []
        for d in range(self.groups):
            for e in reversed(range(count)):
                near = jnp.broadcast_to(here[e][d : d + 1, :], (width, tokens))
                far = jnp.broadcast_to(before[e][d : d + 1, :], (width, tokens))
                tile = pltpu.roll(
                    jnp.where(self.inside, near, far), 0, 1, stride=1, stride_axis=0
                )
                parts.append(tile.astype(jnp.bfloat16))
        return jnp.concatenate(parts, axis=0)

    def windows(self, value):
        previous = self.down(value)
        views = []
        for b in range(self.count):
            back = self.count - 1 - b
            kept = jnp.where(self.piece < self.count - back, value, previous)
            views.append(self.turn(kept, back))
        return views


def layer_kernel(
    groups, lanes, parts, signal_ref, filter_ref, skip_ref, weight_ref, out_ref,
    raw, stage, gains, recv, source, taps, result, padded, values, gathered, held, left, total,
    load_sem, split_send, split_recv, seq_send, seq_recv,
    chan_send, chan_recv,
):
    me = lax.axis_index("seq")
    lane = lax.axis_index("chan")
    part, tokens = signal_ref.shape[2:]
    own = parts * part
    others = [lax.rem(lane + j, lanes) for j in range(1, lanes)]
    partners = [lax.rem(me + k, groups) for k in range(1, groups)]

    filter_load = pltpu.make_async_copy(filter_ref, raw, load_sem.at[0])
    skip_load = pltpu.make_async_copy(skip_ref, gains, load_sem.at[1])
    weight_load = pltpu.make_async_copy(weight_ref, held, load_sem.at[2])
    signal_loads = [
        pltpu.make_async_copy(signal_ref.at[:, h], stage.at[h, :, 0], load_sem.at[3 + h])
        for h in range(parts)
    ]
    filter_load.start()
    for load in signal_loads:
        load.start()
    skip_load.start()
    greet(
        [{"seq": peer} for peer in partners]
        + [{"chan": other} for other in others]
    )
    sent = []

    def push(origin, target, send_sem, recv_sem, device):
        copy = pltpu.make_async_remote_copy(
            src_ref=origin,
            dst_ref=target,
            send_sem=send_sem,
            recv_sem=recv_sem,
            device_id=device,
            device_id_type=MESH,
        )
        copy.start()
        sent.append(copy)
        return copy

    def split(h):
        return [
            push(
                stage.at[h, peer], recv.at[h, k + 1], split_send.at[h, k], split_recv.at[h, k],
                {"seq": peer},
            )
            for k, peer in enumerate(partners)
        ]

    tools = Toeplitz(groups, tokens, tokens // SHARE)

    def unpack(h):
        for k in range(groups):
            place = lax.rem(me - k + groups, groups)
            rows = pl.ds(pl.multiple_of(place * part, part), part)
            source[rows, :] = recv[h, k, 0].astype(jnp.float32)
            taps[rows, :] = recv[h, k, 1].astype(jnp.float32)

    def convolve(h, begin, end):
        def picks_of(first):
            return [pl.ds(first + g, groups, stride=part) for g in range(SHARE)]

        def rows_of(inputs, room):
            for g in range(SHARE):
                for b, view in enumerate(tools.windows(inputs[g])):
                    padded[room, g * SHARE + b, groups:, :] = view
            return jnp.concatenate(
                [
                    padded[room, :, groups - d : 2 * groups - d, :]
                    .reshape(SHARE * SHARE * groups, tokens)
                    .astype(jnp.bfloat16)
                    for d in range(groups)
                ],
                axis=1,
            )

        def turn(step, carry):
            firsts = [(step * ROOMS + room) * SHARE for room in range(ROOMS)]
            picks = [picks_of(first) for first in firsts]
            inputs = [[source[pick, :] for pick in several] for several in picks]
            rows = jnp.concatenate(
                [rows_of(inputs[room], room) for room in range(ROOMS)], axis=0
            )
            columns = jnp.concatenate(
                [
                    tools.matrix([taps[pick, :] for pick in picks[room]])
                    for room in range(ROOMS)
                ],
                axis=1,
            )
            product = jnp.dot(rows, columns, preferred_element_type=jnp.float32)
            height = SHARE * SHARE * groups
            for room in range(ROOMS):
                both = product[
                    room * height : (room + 1) * height, room * tokens : (room + 1) * tokens
                ].reshape(SHARE, SHARE, groups, tokens)
                base = me * own + h * part + firsts[room]
                for g, pick in enumerate(picks[room]):
                    joined = tools.gather(lambda b, g=g: tools.turn(both[g, b], b - g))
                    result[pick, :] = joined + gains[base + g] * inputs[room][g]
            return carry

        lax.fori_loop(begin, end, turn, 0)

    def pack(h):
        for k in range(groups):
            values[h, k] = result[k * part : (k + 1) * part, :].astype(values.dtype)

    def slot(h, which, at):
        return gathered.at[h, which, at]

    def send_values(h):
        copies = [
            push(
                values.at[h, peer], slot(h, lane, me), seq_send.at[h, k], seq_recv.at[h, k],
                {"seq": peer},
            )
            for k, peer in enumerate(partners)
        ]
        gathered[h, lane, me] = values[h, me]
        return copies

    def hand(h, which, send_sem, recv_sem, device):
        row = gathered.at[h, which]
        return push(row, row, send_sem, recv_sem, device)

    def spread(h, arrivals):
        for copy in arrivals:
            copy.wait_recv()
        row = gathered.at[h, lane]
        return [
            push(row, row, chan_send.at[h, j], chan_recv.at[h, j], {"chan": other})
            for j, other in enumerate(others)
        ]

    wide = 512 if out_ref.shape[1] % 512 == 0 else out_ref.shape[1]
    tiles = out_ref.shape[1] // wide
    depth = lanes * groups * part

    def settle(h, inside):
        for copy in inside:
            copy.wait_recv()
        left[...] = gathered[h].reshape(depth, tokens).T

    def project(h, begin, end):
        def tile(step, carry):
            columns = pl.ds(pl.multiple_of(step * wide, wide), wide)
            block = held[:, h * part : (h + 1) * part, columns].reshape(depth, wide)
            amount = jnp.dot(left[...], block, preferred_element_type=jnp.float32)
            if h:
                amount = amount + total[:, columns]
            if h == parts - 1:
                out_ref[:, columns] = amount.astype(out_ref.dtype)
            else:
                total[:, columns] = amount
            return carry

        lax.fori_loop(begin, end, tile, 0)

    filter_load.wait()
    stage[:, :, 1] = jnp.swapaxes(raw[...].astype(stage.dtype), 0, 1)
    signal_loads[0].wait()
    incoming = [split(0)]
    skip_load.wait()
    padded[:, :, :groups, :] = jnp.zeros((ROOMS, SHARE * SHARE, groups, tokens), jnp.float32)
    if parts > 1:
        signal_loads[1].wait()
        incoming.append(split(1))
    weight_load.start()
    turns = part // (SHARE * ROOMS)
    arrivals, inside = [], []
    for h in range(parts):
        recv[h, 0] = stage[h, me]
        for copy in incoming[h]:
            copy.wait_recv()
        if h + 2 < parts:
            signal_loads[h + 2].wait()
            incoming.append(split(h + 2))
        unpack(h)
        convolve(h, 0, turns)
        pack(h)
        arrivals.append(send_values(h))
        if h == 1:
            weight_load.wait()
        if h >= 1:
            inside.append(spread(h - 1, arrivals[h - 1]))
        if h >= 2 and h < parts - 1:
            settle(h - 2, inside[h - 2])
            project(h - 2, 0, tiles)
    last = parts - 1
    if last == 0:
        weight_load.wait()
    if last >= 2:
        settle(last - 2, inside[last - 2])
        project(last - 2, 0, tiles)
    inside.append(spread(last, arrivals[last]))
    if last >= 1:
        settle(last - 1, inside[last - 1])
        project(last - 1, 0, tiles)
    settle(last, inside[last])
    project(last, 0, tiles)
    for copy in sent:
        copy.wait_send()


def per_device(signal, filters, skip, weight):
    groups = lax.axis_size("seq")
    lanes = lax.axis_size("chan")
    channels, tokens = signal.shape
    features = weight.shape[1]
    own = channels // groups
    parts = PARTS if own % (16 * PARTS) == 0 else 1
    part = own // parts
    half, full = jnp.bfloat16, jnp.float32
    dma = pltpu.SemaphoreType.DMA
    whole = pl.BlockSpec(memory_space=pltpu.HBM)
    return pl.pallas_call(
        functools.partial(layer_kernel, groups, lanes, parts),
        out_shape=jax.ShapeDtypeStruct((tokens, features), half),
        in_specs=[whole] * 4,
        out_specs=VMEM,
        scratch_shapes=[
            pltpu.VMEM((groups, parts, part, tokens), full),
            pltpu.VMEM((parts, groups, 2, part, tokens), half),
            pltpu.SMEM((channels,), full),
            pltpu.VMEM((parts, groups, 2, part, tokens), half),
            pltpu.VMEM((groups * part, tokens), full),
            pltpu.VMEM((groups * part, tokens), full),
            pltpu.VMEM((groups * part, tokens), full),
            pltpu.VMEM((ROOMS, SHARE * SHARE, 2 * groups, tokens), full),
            pltpu.VMEM((parts, groups, part, tokens), half),
            pltpu.VMEM((parts, lanes, groups, part, tokens), half),
            pltpu.VMEM((lanes * groups, own, features), half),
            pltpu.VMEM((tokens, lanes * groups * part), half),
            pltpu.VMEM((tokens, features), full),
            dma((3 + parts,)),
            dma((parts, groups - 1)),
            dma((parts, groups - 1)),
            dma((parts, groups - 1)),
            dma((parts, groups - 1)),
            dma((parts, lanes - 1)),
            dma((parts, lanes - 1)),
        ],
        compiler_params=pltpu.CompilerParams(
            collective_id=0, has_side_effects=True, vmem_limit_bytes=LIMIT
        ),
    )(
        signal.reshape(groups, parts, part, tokens),
        filters.reshape(groups, parts, part, tokens),
        skip,
        weight.reshape(lanes * groups, own, features),
    )


def solution(mesh):
    in_specs = (P("chan", "seq"), P("chan", "seq"), P("chan"), P(None, "chan"))
    out_specs = P("seq", "chan")
    return jax.shard_map(
        per_device, mesh=mesh, in_specs=in_specs, out_specs=out_specs, check_vma=False
    )
```

```python
import functools

import jax
import jax.numpy as jnp
from jax import lax
from jax.experimental import pallas as pl
from jax.experimental.pallas import tpu as pltpu
from jax.sharding import PartitionSpec as P

MESH = pl.DeviceIdType.MESH
VMEM = pl.BlockSpec(memory_space=pltpu.VMEM)
PARTS = 2
SHARE = 4
ROOMS = 2
LIMIT = 64 * 1024 * 1024


def greet(peers):
    barrier = pltpu.get_barrier_semaphore()
    for peer in peers:
        pl.semaphore_signal(barrier, inc=1, device_id=peer, device_id_type=MESH)
    pl.semaphore_wait(barrier, len(peers))


class Toeplitz:
    def __init__(self, groups, tokens, width):
        self.groups, self.tokens = groups, tokens
        self.width, self.count = width, tokens // width
        row = lax.broadcasted_iota(jnp.int32, (width, tokens), 0)
        lane = lax.broadcasted_iota(jnp.int32, (width, tokens), 1)
        self.inside = lax.rem(lane, width) < width - row
        self.lane = lax.broadcasted_iota(jnp.int32, (groups, tokens), 1)
        self.piece = self.lane // width
        self.row = lax.broadcasted_iota(jnp.int32, (groups, tokens), 0)

    def turn(self, value, pieces):
        pieces = pieces % self.count
        return pltpu.roll(value, pieces * self.width, 1) if pieces else value

    def gather(self, pick):
        value = pick(0)
        for p in range(1, self.count):
            value = jnp.where(self.piece == p, pick(p), value)
        return value

    def down(self, value):
        return jnp.where(self.row >= 1, pltpu.roll(value, 1, 0), 0.0)

    def matrix(self, taps):
        count, width, tokens = self.count, self.width, self.tokens
        here = [
            self.gather(lambda g, e=e: self.turn(taps[g], g - e)) for e in range(count)
        ]
        following = [self.turn(value, -1) for value in here]
        before = [self.down(following[-1])] + following[:-1]
        parts = []
        for d in range(self.groups):
            for e in reversed(range(count)):
                near = jnp.broadcast_to(here[e][d : d + 1, :], (width, tokens))
                far = jnp.broadcast_to(before[e][d : d + 1, :], (width, tokens))
                tile = pltpu.roll(
                    jnp.where(self.inside, near, far), 0, 1, stride=1, stride_axis=0
                )
                parts.append(tile.astype(jnp.bfloat16))
        return jnp.concatenate(parts, axis=0)

    def windows(self, value):
        previous = self.down(value)
        views = []
        for b in range(self.count):
            back = self.count - 1 - b
            kept = jnp.where(self.piece < self.count - back, value, previous)
            views.append(self.turn(kept, back))
        return views


def layer_kernel(
    groups, lanes, parts, signal_ref, filter_ref, skip_ref, weight_ref, out_ref,
    raw, stage, gains, recv, source, taps, result, padded, values, gathered, held, left, total,
    load_sem, split_send, split_recv, seq_send, seq_recv,
    chan_send, chan_recv,
):
    me = lax.axis_index("seq")
    lane = lax.axis_index("chan")
    part, tokens = signal_ref.shape[2:]
    own = parts * part
    others = [lax.rem(lane + j, lanes) for j in range(1, lanes)]
    partners = [lax.rem(me + k, groups) for k in range(1, groups)]

    filter_load = pltpu.make_async_copy(filter_ref, raw, load_sem.at[0])
    skip_load = pltpu.make_async_copy(skip_ref, gains, load_sem.at[1])
    weight_load = pltpu.make_async_copy(weight_ref, held, load_sem.at[2])
    signal_loads = [
        pltpu.make_async_copy(signal_ref.at[:, h], stage.at[h, :, 0], load_sem.at[3 + h])
        for h in range(parts)
    ]
    filter_load.start()
    for load in signal_loads:
        load.start()
    skip_load.start()
    greet(
        [{"seq": peer} for peer in partners]
        + [{"chan": other} for other in others]
    )
    sent = []

    def push(origin, target, send_sem, recv_sem, device):
        copy = pltpu.make_async_remote_copy(
            src_ref=origin,
            dst_ref=target,
            send_sem=send_sem,
            recv_sem=recv_sem,
            device_id=device,
            device_id_type=MESH,
        )
        copy.start()
        sent.append(copy)
        return copy

    def split(h):
        return [
            push(
                stage.at[h, peer], recv.at[h, k + 1], split_send.at[h, k], split_recv.at[h, k],
                {"seq": peer},
            )
            for k, peer in enumerate(partners)
        ]

    tools = Toeplitz(groups, tokens, tokens // SHARE)

    def unpack(h):
        for k in range(groups):
            place = lax.rem(me - k + groups, groups)
            rows = pl.ds(pl.multiple_of(place * part, part), part)
            source[rows, :] = recv[h, k, 0].astype(jnp.float32)
            taps[rows, :] = recv[h, k, 1].astype(jnp.float32)

    def convolve(h, begin, end):
        def picks_of(first):
            return [pl.ds(first + g, groups, stride=part) for g in range(SHARE)]

        def rows_of(inputs, room):
            for g in range(SHARE):
                for b, view in enumerate(tools.windows(inputs[g])):
                    padded[room, g * SHARE + b, groups:, :] = view
            return jnp.concatenate(
                [
                    padded[room, :, groups - d : 2 * groups - d, :]
                    .reshape(SHARE * SHARE * groups, tokens)
                    .astype(jnp.bfloat16)
                    for d in range(groups)
                ],
                axis=1,
            )

        def turn(step, carry):
            firsts = [(step * ROOMS + room) * SHARE for room in range(ROOMS)]
            picks = [picks_of(first) for first in firsts]
            inputs = [[source[pick, :] for pick in several] for several in picks]
            rows = jnp.concatenate(
                [rows_of(inputs[room], room) for room in range(ROOMS)], axis=0
            )
            columns = jnp.concatenate(
                [
                    tools.matrix([taps[pick, :] for pick in picks[room]])
                    for room in range(ROOMS)
                ],
                axis=1,
            )
            product = jnp.dot(rows, columns, preferred_element_type=jnp.float32)
            height = SHARE * SHARE * groups
            for room in range(ROOMS):
                both = product[
                    room * height : (room + 1) * height, room * tokens : (room + 1) * tokens
                ].reshape(SHARE, SHARE, groups, tokens)
                base = me * own + h * part + firsts[room]
                for g, pick in enumerate(picks[room]):
                    joined = tools.gather(lambda b, g=g: tools.turn(both[g, b], b - g))
                    result[pick, :] = joined + gains[base + g] * inputs[room][g]
            return carry

        lax.fori_loop(begin, end, turn, 0)

    def pack(h):
        for k in range(groups):
            values[h, k] = result[k * part : (k + 1) * part, :].astype(values.dtype)

    def slot(h, which, at):
        return gathered.at[h, which, at]

    def send_values(h):
        copies = [
            push(
                values.at[h, peer], slot(h, lane, me), seq_send.at[h, k], seq_recv.at[h, k],
                {"seq": peer},
            )
            for k, peer in enumerate(partners)
        ]
        gathered[h, lane, me] = values[h, me]
        return copies

    def hand(h, which, send_sem, recv_sem, device):
        row = gathered.at[h, which]
        return push(row, row, send_sem, recv_sem, device)

    def spread(h, arrivals):
        for copy in arrivals:
            copy.wait_recv()
        row = gathered.at[h, lane]
        return [
            push(row, row, chan_send.at[h, j], chan_recv.at[h, j], {"chan": other})
            for j, other in enumerate(others)
        ]

    wide = 512 if out_ref.shape[1] % 512 == 0 else out_ref.shape[1]
    tiles = out_ref.shape[1] // wide
    depth = lanes * groups * part

    def settle(h, inside):
        for copy in inside:
            copy.wait_recv()
        left[...] = gathered[h].reshape(depth, tokens).T

    def project(h, begin, end):
        def tile(step, carry):
            columns = pl.ds(pl.multiple_of(step * wide, wide), wide)
            block = held[:, h * part : (h + 1) * part, columns].reshape(depth, wide)
            amount = jnp.dot(left[...], block, preferred_element_type=jnp.float32)
            if h:
                amount = amount + total[:, columns]
            if h == parts - 1:
                out_ref[:, columns] = amount.astype(out_ref.dtype)
            else:
                total[:, columns] = amount
            return carry

        lax.fori_loop(begin, end, tile, 0)

    filter_load.wait()
    stage[:, :, 1] = jnp.swapaxes(raw[...].astype(stage.dtype), 0, 1)
    signal_loads[0].wait()
    incoming = [split(0)]
    skip_load.wait()
    padded[:, :, :groups, :] = jnp.zeros((ROOMS, SHARE * SHARE, groups, tokens), jnp.float32)
    if parts > 1:
        signal_loads[1].wait()
        incoming.append(split(1))
    weight_load.start()
    turns = part // (SHARE * ROOMS)
    arrivals, inside = [], []
    for h in range(parts):
        recv[h, 0] = stage[h, me]
        for copy in incoming[h]:
            copy.wait_recv()
        if h + 2 < parts:
            signal_loads[h + 2].wait()
            incoming.append(split(h + 2))
        unpack(h)
        convolve(h, 0, turns // 2)
        if h:
            inside.append(spread(h - 1, arrivals[h - 1]))
        convolve(h, turns // 2, turns)
        pack(h)
        arrivals.append(send_values(h))
        if h == 1:
            weight_load.wait()
        if h:
            settle(h - 1, inside[h - 1])
            project(h - 1, 0, tiles // 2 if h == parts - 1 else tiles)
    last = parts - 1
    inside.append(spread(last, arrivals[last]))
    if last:
        project(last - 1, tiles // 2, tiles)
    else:
        weight_load.wait()
    settle(last, inside[last])
    project(last, 0, tiles)
    for copy in sent:
        copy.wait_send()


def per_device(signal, filters, skip, weight):
    groups = lax.axis_size("seq")
    lanes = lax.axis_size("chan")
    channels, tokens = signal.shape
    features = weight.shape[1]
    own = channels // groups
    parts = PARTS if own % (16 * PARTS) == 0 else 1
    part = own // parts
    half, full = jnp.bfloat16, jnp.float32
    dma = pltpu.SemaphoreType.DMA
    whole = pl.BlockSpec(memory_space=pltpu.HBM)
    return pl.pallas_call(
        functools.partial(layer_kernel, groups, lanes, parts),
        out_shape=jax.ShapeDtypeStruct((tokens, features), half),
        in_specs=[whole] * 4,
        out_specs=VMEM,
        scratch_shapes=[
            pltpu.VMEM((groups, parts, part, tokens), full),
            pltpu.VMEM((parts, groups, 2, part, tokens), half),
            pltpu.SMEM((channels,), full),
            pltpu.VMEM((parts, groups, 2, part, tokens), half),
            pltpu.VMEM((groups * part, tokens), full),
            pltpu.VMEM((groups * part, tokens), full),
            pltpu.VMEM((groups * part, tokens), full),
            pltpu.VMEM((ROOMS, SHARE * SHARE, 2 * groups, tokens), full),
            pltpu.VMEM((parts, groups, part, tokens), half),
            pltpu.VMEM((parts, lanes, groups, part, tokens), half),
            pltpu.VMEM((lanes * groups, own, features), half),
            pltpu.VMEM((tokens, lanes * groups * part), half),
            pltpu.VMEM((tokens, features), full),
            dma((3 + parts,)),
            dma((parts, groups - 1)),
            dma((parts, groups - 1)),
            dma((parts, groups - 1)),
            dma((parts, groups - 1)),
            dma((parts, lanes - 1)),
            dma((parts, lanes - 1)),
        ],
        compiler_params=pltpu.CompilerParams(
            collective_id=0, has_side_effects=True, vmem_limit_bytes=LIMIT
        ),
    )(
        signal.reshape(groups, parts, part, tokens),
        filters.reshape(groups, parts, part, tokens),
        skip,
        weight.reshape(lanes * groups, own, features),
    )


def solution(mesh):
    in_specs = (P("chan", "seq"), P("chan", "seq"), P("chan"), P(None, "chan"))
    out_specs = P("seq", "chan")
    return jax.shard_map(
        per_device, mesh=mesh, in_specs=in_specs, out_specs=out_specs, check_vma=False
    )
```
